32 devices in a mesh: fsdp: 8 (over z, core), tp: 4 (over y, x).
Axes of the slice: x: 2, y: 2, z: 4, core: 2. Of those that a mesh axis runs over, the one named last changes fastest.
Arguments:
- states: bfloat16 [256, 4, 8192], P('fsdp'), may hold values from -6 to 6
- norm_gain: float32 [8192], replicated, may hold values from 0.5 to 1.5
- query_base: bfloat16 [8192, 8192], P(('fsdp', 'tp')), may hold values from -0.0625 to 0.0625
- key_base: bfloat16 [8192, 1024], P(('fsdp', 'tp')), may hold values from -0.0625 to 0.0625
- value_base: bfloat16 [8192, 1024], P(('fsdp', 'tp')), may hold values from -0.0625 to 0.0625
- output_base: bfloat16 [8192, 8192], P(('fsdp', 'tp')), may hold values from -0.5 to 0.5
- query_down: bfloat16 [4, 8192, 64], P(None, ('fsdp', 'tp')), may hold values from -0.0625 to 0.0625
- query_up: bfloat16 [4, 64, 8192], replicated, may hold values from -0.75 to 0.75
- key_down: bfloat16 [4, 8192, 64], P(None, ('fsdp', 'tp')), may hold values from -0.0625 to 0.0625
- key_up: bfloat16 [4, 64, 1024], replicated, may hold values from -0.75 to 0.75
- value_down: bfloat16 [4, 8192, 64], P(None, ('fsdp', 'tp')), may hold values from -0.0625 to 0.0625
- value_up: bfloat16 [4, 64, 1024], replicated, may hold values from -0.75 to 0.75
- output_down: bfloat16 [4, 8192, 64], P(None, ('fsdp', 'tp')), may hold values from -0.5 to 0.5
- output_up: bfloat16 [4, 64, 8192], replicated, may hold values from -0.75 to 0.75
- adapter_layer: int32 [1], replicated, may hold values from 0 to 3
- kv_lengths: int32 [256], P('fsdp'), may hold values from 8 to 512
- cache_keys: bfloat16 [256, 512, 8, 128], P('fsdp', None, 'tp'), may hold values from -320 to 320
- cache_values: bfloat16 [256, 512, 8, 128], P('fsdp', None, 'tp'), may hold values from -6 to 6
Outputs:
- layer_update: bfloat16 [256, 4, 8192], P('fsdp', None, 'tp')
The draws below stay inside these ranges and needn't reach their ends.
Inputs may be any that keep to these rules, and one draw needn't show every extreme that they name: `kv_lengths`: slots at and beyond a sequence's length hold no cached position.
All inputs are finite; a program needn't handle non-finite values.
Results may differ from the reference program's by a relative error of at most 0.012.
The reference program's roundings to bfloat16 on the way count: a program that leaves them out, or rounds other values in their place, can miss the bound.
Values may be sent and summed in bfloat16 or wider, within the bound.
No kernel may reach another device: no remote copies, remote signals or barrier semaphores. Data moves between devices by JAX's collectives and lax.ppermute only.
A program may use at most 128 MiB of HBM per device.

```python
import jax
import jax.numpy as jnp
from jax import lax

D = 8192
HQ = 64
KVH = 8
DH = 128
R = 64
SLOTS = 4
STEPS = 4
SEQ_DEV = 32
LEN = 512
SEQS = 256
N_FSDP = 8


def draw_cache_keys(key, part):
    array_shape = (SEQS, LEN, KVH, DH)
    standard = jnp.clip(jax.random.normal(jax.random.fold_in(key, 11), array_shape, jnp.float32), -4.0, 4.0)
    return standard.astype(jnp.bfloat16)


def plant(array, key, least, high):
    place = [jax.random.randint(jax.random.fold_in(key, axis), (), 0, length) for axis, length in enumerate(array.shape)]
    longest = array.shape.index(max(array.shape))
    beside = place[:longest] + [(place[longest] + 1) % array.shape[longest]] + place[longest + 1:]
    return array.at[tuple(place)].set(least).at[tuple(beside)].set(high)


def steps_of(rng, extent, cuts, least, high):
    gain = 1.0
    for dim, parts in cuts:
        heights = jax.random.uniform(jax.random.fold_in(jax.random.fold_in(rng, 6), dim), (parts,), jnp.float32, least / len(cuts), high / len(cuts))
        gain = gain * jnp.repeat(jnp.exp(heights), extent[dim] // parts).reshape((-1,) + (1,) * (len(extent) - 1 - dim))
    return gain


def scatter_about(rng, extent, scale, limit, cuts=(), kind=jnp.bfloat16):
    factor_of = steps_of(rng, extent, cuts, -0.22, 0.18) if cuts else 1.0
    result = jax.random.normal(rng, extent, jnp.float32) * scale * factor_of
    return jnp.minimum(jnp.maximum(result, -limit), limit).astype(kind)


def setup_inputs(seed: int = 0) -> dict:
    streams_of = jax.random.split(jax.random.key(seed), 19)
    states = scatter_about(streams_of[0], (SEQS, STEPS, D), 1.0, 6.0, ((0, 8),))
    norm_gain = jnp.clip(1.0 + 0.1 * jax.random.normal(streams_of[1], (D,), jnp.float32), 0.5, 1.5)
    query_base = scatter_about(streams_of[2], (D, HQ * DH), D ** -0.5, 0.0625, ((0, 32),))
    key_base = scatter_about(streams_of[3], (D, KVH * DH), D ** -0.5, 0.0625, ((0, 32),))
    value_base = scatter_about(streams_of[4], (D, KVH * DH), D ** -0.5, 0.0625, ((0, 32),))
    output_base = scatter_about(streams_of[5], (HQ * DH, D), (HQ * DH // 64) ** -0.5, 0.5, ((0, 32),))
    query_down = scatter_about(streams_of[6], (SLOTS, D, R), D ** -0.5, 0.0625, ((1, 32),))
    query_up = scatter_about(streams_of[7], (SLOTS, R, HQ * DH), R ** -0.5, 0.75)
    key_down = scatter_about(streams_of[8], (SLOTS, D, R), D ** -0.5, 0.0625, ((1, 32),))
    key_up = scatter_about(streams_of[9], (SLOTS, R, KVH * DH), R ** -0.5, 0.75)
    value_down = scatter_about(streams_of[10], (SLOTS, D, R), D ** -0.5, 0.0625, ((1, 32),))
    value_up = scatter_about(streams_of[11], (SLOTS, R, KVH * DH), R ** -0.5, 0.75)
    output_down = scatter_about(streams_of[12], (SLOTS, HQ * DH, R), (HQ * DH // 64) ** -0.5, 0.5, ((1, 32),))
    output_up = scatter_about(streams_of[13], (SLOTS, R, D), R ** -0.5, 0.75)
    adapter_layer = jax.random.randint(streams_of[14], (1,), 0, SLOTS).astype(jnp.int32)
    kv_lengths = plant(jax.random.randint(streams_of[15], (SEQS,), 8, LEN + 1), jax.random.fold_in(streams_of[15], 1), 8, LEN).astype(jnp.int32)
    cache_keys = draw_cache_keys(jax.random.fold_in(streams_of[18], 71), 0)
    cache_values = scatter_about(streams_of[17], (SEQS, LEN, KVH, DH), 1.0, 6.0, ((0, 8), (2, 4)))
    return dict(states=states, norm_gain=norm_gain, query_base=query_base, key_base=key_base, value_base=value_base, output_base=output_base, query_down=query_down, query_up=query_up, key_down=key_down, key_up=key_up, value_down=value_down, value_up=value_up, output_down=output_down, output_up=output_up, adapter_layer=adapter_layer, kv_lengths=kv_lengths, cache_keys=cache_keys, cache_values=cache_values)


rope_theta = 1000000.0
low_rank_scale = 0.5
epsilon = 1e-06

def merge_rows(frozen_base_rows, down_stack, up_stack, adapter_slot):
    down_rows = lax.dynamic_index_in_dim(down_stack, adapter_slot, 0, keepdims=False)
    up_projection_rows = lax.dynamic_index_in_dim(up_stack, adapter_slot, 0, keepdims=False)
    low_rank_delta = jnp.dot(down_rows, up_projection_rows, preferred_element_type=jnp.float32)
    return (frozen_base_rows.astype(jnp.float32) + low_rank_scale * low_rank_delta).astype(jnp.bfloat16)

def normalize(states, norm_gain):
    widened = states.astype(jnp.float32)
    squared_average = lax.optimization_barrier(jnp.mean(widened * widened, axis=-1, keepdims=True))
    return (widened * lax.rsqrt(squared_average + epsilon) * norm_gain).astype(jnp.bfloat16)

def rotate(vectors, positions):
    head_dim = vectors.shape[-1]
    half_dim = head_dim // 2
    frequency = rope_theta ** (-2.0 * jnp.arange(half_dim, dtype=jnp.float32) / head_dim)
    rotation_phases = positions[:, :, None] * frequency[None, None, :]
    cosine_table = jnp.concatenate((jnp.cos(rotation_phases), jnp.cos(rotation_phases)), -1)[:, :, None, :]
    sine_table = jnp.concatenate((jnp.sin(rotation_phases), jnp.sin(rotation_phases)), -1)[:, :, None, :]
    turned = jnp.concatenate((-vectors[..., half_dim:], vectors[..., :half_dim]), -1)
    return vectors * cosine_table + turned * sine_table

def attend_block(inputs):
    queries, keys_new, values_new, cache_k, cache_v, lengths = inputs
    seq_count, step_count, head_count, head_dim = queries.shape
    kv_count = keys_new.shape[2]
    grouped = queries.astype(jnp.float32).reshape(seq_count, step_count, kv_count, head_count // kv_count, head_dim)
    score_scale = head_dim ** (-0.5)
    old_scores = jnp.einsum('bskgd,blkd->bskgl', grouped, cache_k.astype(jnp.float32)) * score_scale
    new_scores = jnp.einsum('bskgd,btkd->bskgt', grouped, keys_new.astype(jnp.float32)) * score_scale
    live_slots = jnp.arange(cache_k.shape[1], dtype=jnp.int32)[None, :] < lengths[:, None]
    old_scores = jnp.where(live_slots[:, None, None, None, :], old_scores, -1e+30)
    causal = jnp.arange(step_count)[:, None] >= jnp.arange(step_count)[None, :]
    new_scores = jnp.where(causal[None, :, None, None, :], new_scores, -1e+30)
    highest = jnp.maximum(lax.optimization_barrier(jnp.max(old_scores, -1)), lax.optimization_barrier(jnp.max(new_scores, -1)))[..., None]
    old_exp = jnp.exp(old_scores - highest)
    new_exp = jnp.exp(new_scores - highest)
    denominator = lax.optimization_barrier(jnp.sum(old_exp, -1, keepdims=True)) + lax.optimization_barrier(jnp.sum(new_exp, -1, keepdims=True))
    old_weights = (old_exp / denominator).astype(jnp.bfloat16)
    new_weights = (new_exp / denominator).astype(jnp.bfloat16)
    mixture = jnp.einsum('bskgl,blkd->bskgd', old_weights.astype(jnp.float32), cache_v.astype(jnp.float32))
    mixture = mixture + jnp.einsum('bskgt,btkd->bskgd', new_weights.astype(jnp.float32), values_new.astype(jnp.float32))
    return mixture.astype(jnp.bfloat16).reshape(seq_count, step_count, head_count * head_dim)

def blockwise(tensor):
    return tensor.reshape((N_FSDP, SEQ_DEV) + tensor.shape[1:])

def reference(states, norm_gain, query_base, key_base, value_base, output_base, query_down, query_up, key_down, key_up, value_down, value_up, output_down, output_up, adapter_layer, kv_lengths, cache_keys, cache_values):
    adapter_slot = adapter_layer[0]
    merged_query = merge_rows(query_base, query_down, query_up, adapter_slot)
    merged_key = merge_rows(key_base, key_down, key_up, adapter_slot)
    merged_value = merge_rows(value_base, value_down, value_up, adapter_slot)
    merged_output = merge_rows(output_base, output_down, output_up, adapter_slot)
    normed = normalize(states, norm_gain)
    flat_rows = normed.reshape(SEQS * STEPS, D)
    positions = kv_lengths.astype(jnp.float32)[:, None] + jnp.arange(STEPS, dtype=jnp.float32)[None, :]
    queries = jnp.dot(flat_rows, merged_query, preferred_element_type=jnp.float32).reshape(SEQS, STEPS, HQ, DH)
    queries = rotate(queries, positions).astype(jnp.bfloat16)
    keys_new = jnp.dot(flat_rows, merged_key, preferred_element_type=jnp.float32).reshape(SEQS, STEPS, KVH, DH)
    keys_new = rotate(keys_new, positions).astype(jnp.bfloat16)
    values_new = jnp.dot(flat_rows, merged_value, preferred_element_type=jnp.float32).reshape(SEQS, STEPS, KVH, DH).astype(jnp.bfloat16)
    attended = lax.map(attend_block, (blockwise(queries), blockwise(keys_new), blockwise(values_new), blockwise(cache_keys), blockwise(cache_values), blockwise(kv_lengths)))
    attended = attended.reshape(SEQS * STEPS, HQ * DH)
    layer_update = jnp.dot(attended, merged_output, preferred_element_type=jnp.float32)
    return layer_update.reshape(SEQS, STEPS, D).astype(jnp.bfloat16)
```

```python
import jax
import jax.numpy as jnp
from jax import lax
from jax.sharding import Mesh, PartitionSpec as P

HQ = 64
KVH = 8
DH = 128

rope_theta = 1000000.0
low_rank_scale = 0.5
epsilon = 1e-06
CHUNKS = 1


def merge_rows(base, down_stack, up_stack, slot):
    down = lax.dynamic_index_in_dim(down_stack, slot, 0, keepdims=False)
    up = lax.dynamic_index_in_dim(up_stack, slot, 0, keepdims=False)
    delta = jnp.dot(down, up, preferred_element_type=jnp.float32)
    return (base.astype(jnp.float32) + low_rank_scale * delta).astype(jnp.bfloat16)


def normalize(states, norm_gain):
    widened = states.astype(jnp.float32)
    squared_average = jnp.mean(widened * widened, axis=-1, keepdims=True)
    return (widened * lax.rsqrt(squared_average + epsilon) * norm_gain).astype(jnp.bfloat16)


def rotate(vectors, positions):
    head_dim = vectors.shape[-1]
    half_dim = head_dim // 2
    frequency = rope_theta ** (-2.0 * jnp.arange(half_dim, dtype=jnp.float32) / head_dim)
    phases = positions[:, :, None] * frequency[None, None, :]
    cosine = jnp.concatenate((jnp.cos(phases), jnp.cos(phases)), -1)[:, :, None, :]
    sine = jnp.concatenate((jnp.sin(phases), jnp.sin(phases)), -1)[:, :, None, :]
    turned = jnp.concatenate((-vectors[..., half_dim:], vectors[..., :half_dim]), -1)
    return vectors * cosine + turned * sine


def attend(queries, keys_new, values_new, cache_k, cache_v, lengths):
    seq_count, step_count, head_count, head_dim = queries.shape
    kv_count = keys_new.shape[2]
    grouped = queries.reshape(seq_count, step_count, kv_count, head_count // kv_count, head_dim)
    score_scale = head_dim ** (-0.5)
    old_scores = (
        jnp.einsum("bskgd,blkd->bskgl", grouped, cache_k, preferred_element_type=jnp.float32)
        * score_scale
    )
    new_scores = (
        jnp.einsum("bskgd,btkd->bskgt", grouped, keys_new, preferred_element_type=jnp.float32)
        * score_scale
    )
    live_slots = jnp.arange(cache_k.shape[1], dtype=jnp.int32)[None, :] < lengths[:, None]
    old_scores = jnp.where(live_slots[:, None, None, None, :], old_scores, -1e30)
    causal = jnp.arange(step_count)[:, None] >= jnp.arange(step_count)[None, :]
    new_scores = jnp.where(causal[None, :, None, None, :], new_scores, -1e30)
    highest = jnp.maximum(jnp.max(old_scores, -1), jnp.max(new_scores, -1))[..., None]
    old_exp = jnp.exp(old_scores - highest)
    new_exp = jnp.exp(new_scores - highest)
    denominator = jnp.sum(old_exp, -1, keepdims=True) + jnp.sum(new_exp, -1, keepdims=True)
    old_weights = (old_exp / denominator).astype(jnp.bfloat16)
    new_weights = (new_exp / denominator).astype(jnp.bfloat16)
    mixture = jnp.einsum(
        "bskgl,blkd->bskgd", old_weights, cache_v, preferred_element_type=jnp.float32
    )
    mixture = mixture + jnp.einsum(
        "bskgt,btkd->bskgd", new_weights, values_new, preferred_element_type=jnp.float32
    )
    return mixture.astype(jnp.bfloat16).reshape(seq_count * step_count, head_count * head_dim)


def by_xor(blocks, index):
    count = len(blocks)
    bit = 1
    while bit < count:
        odd = (index & bit) != 0
        blocks = [jnp.where(odd, blocks[i ^ bit], blocks[i]) for i in range(count)]
        bit *= 2
    return blocks


def local(
    states,
    norm_gain,
    query_base,
    key_base,
    value_base,
    output_base,
    query_down,
    query_up,
    key_down,
    key_up,
    value_down,
    value_up,
    output_down,
    output_up,
    adapter_layer,
    kv_lengths,
    cache_keys,
    cache_values,
):
    slot = adapter_layer[0]
    planes, cores, cols = lax.axis_size("z"), lax.axis_size("core"), lax.axis_size("tp")
    z, t = lax.axis_index("z"), lax.axis_index("tp")
    core = lax.axis_index("core")
    plane_pairs = [[(a, a ^ k) for a in range(planes)] for k in range(planes)]
    tp_pairs = [[(a, a ^ k) for a in range(cols)] for k in range(cols)]
    core_pairs = [(0, 1), (1, 0)]
    depth = query_base.shape[0]
    seqs, steps, width = states.shape
    rows = seqs * steps

    normed = normalize(states, norm_gain).reshape(rows, width)
    normed = jnp.stack(jnp.split(normed, planes, axis=1))
    mine = []
    for k in range(planes):
        block = lax.dynamic_index_in_dim(normed, z ^ k, 0, keepdims=False)
        mine.append(lax.ppermute(block, "z", plane_pairs[k]) if k else block)
    other = [lax.ppermute(block, "core", core_pairs) for block in mine]

    query = merge_rows(query_base, query_down, query_up, slot).reshape(depth, cols, cores, -1)
    key = merge_rows(key_base, key_down, key_up, slot).reshape(depth, cols, 1, -1)
    value = merge_rows(value_base, value_down, value_up, slot).reshape(depth, cols, 1, -1)
    joined = jnp.concatenate((query, jnp.concatenate((key, value), 2)), 3)
    joined = joined.transpose(2, 1, 0, 3).reshape(cores * cols * depth, -1)
    weights = lax.all_to_all(joined, ("core", "tp"), 0, 0, tiled=True)

    merged_output = merge_rows(output_base, output_down, output_up, slot)
    merged_output = merged_output.reshape(depth, cols, cores, -1).transpose(2, 1, 0, 3)
    merged_output = merged_output.reshape(cores * cols * depth, -1)
    merged_output, weights = lax.optimization_barrier((merged_output, weights))
    output_weights = lax.all_to_all(merged_output, ("core", "tp"), 0, 0, tiled=True)

    half_q = HQ * DH // (cols * cores)
    kv_cols = KVH * DH // cols
    part = rows // CHUNKS
    seq_part = seqs // CHUNKS
    outs = []
    for h in range(CHUNKS):
        sl = slice(h * part, (h + 1) * part)
        total = None
        for k in list(range(1, planes)) + [0]:
            block = jnp.concatenate((mine[k][sl], other[k][sl]))
            product = jnp.dot(block, weights, preferred_element_type=jnp.float32)
            if k:
                product = lax.ppermute(product.astype(jnp.float16), "z", plane_pairs[k])
                product = product.astype(jnp.float32)
            total = product if total is None else total + product
        here = total[:part]
        there = lax.ppermute(total[part:], "core", core_pairs)
        low = jnp.where(core == 0, here, there)
        high = jnp.where(core == 0, there, here)
        lengths = kv_lengths[h * seq_part : (h + 1) * seq_part]
        positions = (
            lengths.astype(jnp.float32)[:, None] + jnp.arange(steps, dtype=jnp.float32)[None, :]
        )
        queries = jnp.concatenate((low[:, :half_q], high[:, :half_q]), 1)
        queries = rotate(queries.reshape(seq_part, steps, -1, DH), positions).astype(jnp.bfloat16)
        keys_new = rotate(low[:, half_q:].reshape(seq_part, steps, -1, DH), positions)
        keys_new = keys_new.astype(jnp.bfloat16)
        values_new = high[:, half_q:].reshape(seq_part, steps, -1, DH).astype(jnp.bfloat16)
        ss = slice(h * seq_part, (h + 1) * seq_part)
        attended = attend(
            queries, keys_new, values_new, cache_keys[ss], cache_values[ss], lengths
        )

        attended = attended.reshape(cols, part // cols, -1)
        turned = []
        for j in range(cols):
            block = lax.dynamic_index_in_dim(attended, t ^ j, 0, keepdims=False)
            turned.append(lax.ppermute(block, "tp", tp_pairs[j]) if j else block)
        turned = jnp.stack(turned)
        heads = []
        for k in range(planes):
            block = lax.dynamic_index_in_dim(turned, t ^ z ^ k, 0, keepdims=False)
            heads.append(lax.ppermute(block, "z", plane_pairs[k]) if k else block)
        heads = jnp.stack(heads)
        gathered = [lax.ppermute(heads, "tp", tp_pairs[j]) if j else heads for j in range(cols)]
        gathered = jnp.stack(gathered, 1).reshape(planes, part, -1)
        crossed = lax.ppermute(gathered, "core", core_pairs)
        total = None
        for k in list(range(1, planes)) + [0]:
            block = jnp.concatenate((gathered[k], crossed[k]))
            product = jnp.dot(block, output_weights, preferred_element_type=jnp.float32)
            if k:
                product = lax.ppermute(product.astype(jnp.bfloat16), "z", plane_pairs[k])
                product = product.astype(jnp.float32)
            total = product if total is None else total + product
        total = total.astype(jnp.bfloat16)
        here = total[:part]
        there = lax.ppermute(total[part:], "core", core_pairs)
        low = jnp.where(core == 0, here, there)
        high = jnp.where(core == 0, there, here)
        full = jnp.concatenate((low, high), 1).reshape(cols, part // cols, -1)
        full = jnp.stack(by_xor([full[j] for j in range(cols)], t))
        outs.append(full.reshape(seq_part, steps, -1))
    return jnp.concatenate(outs)


def solution(mesh):
    tp_size = mesh.shape["tp"]
    fine = Mesh(mesh.devices.reshape(-1, 2, tp_size), ("z", "core", "tp"))
    fsdp = ("z", "core")
    split = ("z", "core", "tp")
    in_specs = (
        P(fsdp, None, None),
        P(),
        P(split, None),
        P(split, None),
        P(split, None),
        P(split, None),
        P(None, split, None),
        P(),
        P(None, split, None),
        P(),
        P(None, split, None),
        P(),
        P(None, split, None),
        P(),
        P(),
        P(fsdp),
        P(fsdp, None, "tp", None),
        P(fsdp, None, "tp", None),
    )
    out_specs = P(fsdp, None, "tp")
    return jax.shard_map(local, mesh=fine, in_specs=in_specs, out_specs=out_specs, check_vma=False)
```

```python
import jax
import jax.numpy as jnp
from jax import lax
from jax.experimental import pallas as pl
from jax.experimental.pallas import tpu as pltpu
from jax.sharding import Mesh, PartitionSpec as P

HQ = 64
KVH = 8
DH = 128

rope_theta = 1000000.0
low_rank_scale = 0.5
epsilon = 1e-06
CHUNKS = 1


def GROUPS(count):
    return [[0]] + [list(range(1, count))]


def merge_block(base, down, up):
    delta = lax.dot_general(
        down, up, (((0,), (0,)), ((), ())), preferred_element_type=jnp.float32
    )
    return (base.astype(jnp.float32) + low_rank_scale * delta).astype(jnp.bfloat16)


def merge_kernel(slot_ref, base_ref, down_ref, up_ref, out_ref):
    cores, _, _, piece = out_ref.shape
    for c in range(cores):
        part = slice(c * piece, (c + 1) * piece)
        out_ref[c, 0] = merge_block(base_ref[:, part], down_ref[0], up_ref[0, :, part])


def merge_input_kernel(
    slot_ref, qb_ref, kb_ref, vb_ref, qd_ref, kd_ref, vd_ref, qu_ref, ku_ref, vu_ref, out_ref
):
    cores = out_ref.shape[0]
    piece = qb_ref.shape[1] // cores
    for c in range(cores):
        part = slice(c * piece, (c + 1) * piece)
        out_ref[c, 0, :, :piece] = merge_block(qb_ref[:, part], qd_ref[0], qu_ref[0, :, part])
    out_ref[0, 0, :, piece:] = merge_block(kb_ref[...], kd_ref[0], ku_ref[0])
    out_ref[1, 0, :, piece:] = merge_block(vb_ref[...], vd_ref[0], vu_ref[0])


def flipped(down):
    return jnp.swapaxes(down, 1, 2)


def merge_output(slot, base, down, up, cores, cols):
    depth, width = base.shape
    rank = up.shape[1]
    piece = width // (cols * cores)
    grid = pltpu.PrefetchScalarGridSpec(
        num_scalar_prefetch=1,
        grid=(cols,),
        in_specs=[
            pl.BlockSpec((depth, piece * cores), lambda t, s: (0, t)),
            pl.BlockSpec((1, rank, depth), lambda t, s: (s[0], 0, 0)),
            pl.BlockSpec((1, rank, piece * cores), lambda t, s: (s[0], 0, t)),
        ],
        out_specs=pl.BlockSpec((cores, 1, depth, piece), lambda t, s: (0, t, 0, 0)),
    )
    return pl.pallas_call(
        merge_kernel,
        grid_spec=grid,
        out_shape=jax.ShapeDtypeStruct((cores, cols, depth, piece), base.dtype),
        cost_estimate=pl.CostEstimate(
            flops=2 * depth * rank * width, bytes_accessed=5 * depth * width, transcendentals=0
        ),
        compiler_params=pltpu.CompilerParams(vmem_limit_bytes=32 * 1024 * 1024),
        name="merge_output",
    )(slot, base, flipped(down), up)


def merge_inputs(slot, bases, downs, ups, cores, cols):
    depth, width = bases[0].shape
    rank = ups[0].shape[1]
    piece = width // (cols * cores)
    side = bases[1].shape[1] // cols
    whole = pl.BlockSpec((1, rank, depth), lambda t, s: (s[0], 0, 0))
    grid = pltpu.PrefetchScalarGridSpec(
        num_scalar_prefetch=1,
        grid=(cols,),
        in_specs=[
            pl.BlockSpec((depth, piece * cores), lambda t, s: (0, t)),
            pl.BlockSpec((depth, side), lambda t, s: (0, t)),
            pl.BlockSpec((depth, side), lambda t, s: (0, t)),
            whole,
            whole,
            whole,
            pl.BlockSpec((1, rank, piece * cores), lambda t, s: (s[0], 0, t)),
            pl.BlockSpec((1, rank, side), lambda t, s: (s[0], 0, t)),
            pl.BlockSpec((1, rank, side), lambda t, s: (s[0], 0, t)),
        ],
        out_specs=pl.BlockSpec((cores, 1, depth, piece + side), lambda t, s: (0, t, 0, 0)),
    )
    return pl.pallas_call(
        merge_input_kernel,
        grid_spec=grid,
        out_shape=jax.ShapeDtypeStruct((cores, cols, depth, piece + side), bases[0].dtype),
        cost_estimate=pl.CostEstimate(
            flops=3 * depth * rank * width, bytes_accessed=6 * depth * width, transcendentals=0
        ),
        compiler_params=pltpu.CompilerParams(vmem_limit_bytes=32 * 1024 * 1024),
        name="merge_inputs",
    )(slot, *bases, *[flipped(d) for d in downs], *ups)


def norm_kernel(z_ref, x_ref, gain_ref, *refs):
    outs, scratch = refs[:-1], refs[-1]
    x = x_ref[...].astype(jnp.float32)
    mean = jnp.mean(x * x, axis=-1, keepdims=True)
    scratch[...] = (x * lax.rsqrt(mean + epsilon) * gain_ref[...]).astype(jnp.bfloat16)
    block = outs[0].shape[1]
    for k, out_ref in enumerate(outs):
        start = pl.multiple_of((z_ref[0] ^ k) * block, block)
        out_ref[...] = scratch[:, pl.ds(start, block)]


def normed_blocks(z, x, gain, planes):
    rows, width = x.shape
    step = min(rows, 32)
    block = width // planes
    grid = pltpu.PrefetchScalarGridSpec(
        num_scalar_prefetch=1,
        grid=(rows // step,),
        in_specs=[
            pl.BlockSpec((step, width), lambda i, z: (i, 0)),
            pl.BlockSpec((1, width), lambda i, z: (0, 0)),
        ],
        out_specs=[pl.BlockSpec((step, block), lambda i, z: (i, 0))] * planes,
        scratch_shapes=[pltpu.VMEM((step, width), jnp.bfloat16)],
    )
    return pl.pallas_call(
        norm_kernel,
        grid_spec=grid,
        out_shape=[jax.ShapeDtypeStruct((rows, block), jnp.bfloat16)] * planes,
        cost_estimate=pl.CostEstimate(
            flops=6 * rows * width, bytes_accessed=4 * rows * width, transcendentals=rows
        ),
        name="normed_blocks",
    )(z.astype(jnp.int32).reshape(1), x, gain.reshape(1, width))


def rotate(vectors, positions):
    head_dim = vectors.shape[-1]
    half_dim = head_dim // 2
    frequency = rope_theta ** (-2.0 * jnp.arange(half_dim, dtype=jnp.float32) / head_dim)
    phases = positions[:, :, None] * frequency[None, None, :]
    cosine = jnp.concatenate((jnp.cos(phases), jnp.cos(phases)), -1)[:, :, None, :]
    sine = jnp.concatenate((jnp.sin(phases), jnp.sin(phases)), -1)[:, :, None, :]
    turned = jnp.concatenate((-vectors[..., half_dim:], vectors[..., :half_dim]), -1)
    return vectors * cosine + turned * sine


def attend(queries, keys_new, values_new, cache_k, cache_v, lengths):
    seq_count, step_count, head_count, head_dim = queries.shape
    kv_count = keys_new.shape[2]
    grouped = queries.reshape(seq_count, step_count, kv_count, head_count // kv_count, head_dim)
    score_scale = head_dim ** (-0.5)
    old_scores = (
        jnp.einsum("bskgd,blkd->bskgl", grouped, cache_k, preferred_element_type=jnp.float32)
        * score_scale
    )
    new_scores = (
        jnp.einsum("bskgd,btkd->bskgt", grouped, keys_new, preferred_element_type=jnp.float32)
        * score_scale
    )
    live_slots = jnp.arange(cache_k.shape[1], dtype=jnp.int32)[None, :] < lengths[:, None]
    old_scores = jnp.where(live_slots[:, None, None, None, :], old_scores, -1e30)
    causal = jnp.arange(step_count)[:, None] >= jnp.arange(step_count)[None, :]
    new_scores = jnp.where(causal[None, :, None, None, :], new_scores, -1e30)
    highest = jnp.maximum(jnp.max(old_scores, -1), jnp.max(new_scores, -1))[..., None]
    old_exp = jnp.exp(old_scores - highest)
    new_exp = jnp.exp(new_scores - highest)
    denominator = jnp.sum(old_exp, -1, keepdims=True) + jnp.sum(new_exp, -1, keepdims=True)
    old_weights = (old_exp / denominator).astype(jnp.bfloat16)
    new_weights = (new_exp / denominator).astype(jnp.bfloat16)
    mixture = jnp.einsum(
        "bskgl,blkd->bskgd", old_weights, cache_v, preferred_element_type=jnp.float32
    )
    mixture = mixture + jnp.einsum(
        "bskgt,btkd->bskgd", new_weights, values_new, preferred_element_type=jnp.float32
    )
    return mixture.astype(jnp.bfloat16).reshape(seq_count * step_count, head_count * head_dim)


def by_xor(blocks, index):
    count = len(blocks)
    bit = 1
    while bit < count:
        odd = (index & bit) != 0
        blocks = [jnp.where(odd, blocks[i ^ bit], blocks[i]) for i in range(count)]
        bit *= 2
    return blocks


def local(
    states,
    norm_gain,
    query_base,
    key_base,
    value_base,
    output_base,
    query_down,
    query_up,
    key_down,
    key_up,
    value_down,
    value_up,
    output_down,
    output_up,
    adapter_layer,
    kv_lengths,
    cache_keys,
    cache_values,
):
    planes, cores, cols = lax.axis_size("z"), lax.axis_size("core"), lax.axis_size("tp")
    z, t = lax.axis_index("z"), lax.axis_index("tp")
    core = lax.axis_index("core")
    plane_pairs = [[(a, a ^ k) for a in range(planes)] for k in range(planes)]
    tp_pairs = [[(a, a ^ k) for a in range(cols)] for k in range(cols)]
    core_pairs = [(0, 1), (1, 0)]
    depth = query_base.shape[0]
    seqs, steps, width = states.shape
    rows = seqs * steps

    blocks = normed_blocks(z, states.reshape(rows, width), norm_gain, planes)
    joined = merge_inputs(
        adapter_layer,
        (query_base, key_base, value_base),
        (query_down, key_down, value_down),
        (query_up, key_up, value_up),
        cores,
        cols,
    )
    (joined, output_base, *blocks) = lax.optimization_barrier((joined, output_base, *blocks))
    joined = joined.reshape(cores * cols * depth, -1)
    weights = lax.all_to_all(joined, ("core", "tp"), 0, 0, tiled=True)
    mine = [lax.ppermute(blocks[k], "z", plane_pairs[k]) for k in range(1, planes)]
    mine = [blocks[0]] + mine
    other = [lax.ppermute(block, "core", core_pairs) for block in mine]
    merged = merge_output(adapter_layer, output_base, output_down, output_up, cores, cols)
    merged = merged.reshape(cores * cols * depth, -1)
    (weights, merged, *both) = lax.optimization_barrier((weights, merged, *mine, *other))
    mine, other = both[:planes], both[planes:]
    output_weights = lax.all_to_all(merged, ("core", "tp"), 0, 0, tiled=True)

    half_q = HQ * DH // (cols * cores)
    kv_cols = KVH * DH // cols
    part = rows // CHUNKS
    seq_part = seqs // CHUNKS
    outs = []
    for h in range(CHUNKS):
        sl = slice(h * part, (h + 1) * part)
        total = None
        for k in list(range(1, planes)) + [0]:
            block = jnp.concatenate((mine[k][sl], other[k][sl]))
            product = jnp.dot(block, weights, preferred_element_type=jnp.float32)
            if k:
                product = lax.ppermute(product.astype(jnp.float16), "z", plane_pairs[k])
                product = product.astype(jnp.float32)
            total = product if total is None else total + product
        if h == 0:
            total, output_weights = lax.optimization_barrier((total, output_weights))
        here = total[:part]
        there = lax.ppermute(total[part:], "core", core_pairs)
        low = jnp.where(core == 0, here, there)
        high = jnp.where(core == 0, there, here)
        lengths = kv_lengths[h * seq_part : (h + 1) * seq_part]
        positions = (
            lengths.astype(jnp.float32)[:, None] + jnp.arange(steps, dtype=jnp.float32)[None, :]
        )
        queries = jnp.concatenate((low[:, :half_q], high[:, :half_q]), 1)
        queries = rotate(queries.reshape(seq_part, steps, -1, DH), positions).astype(jnp.bfloat16)
        keys_new = rotate(low[:, half_q:].reshape(seq_part, steps, -1, DH), positions)
        keys_new = keys_new.astype(jnp.bfloat16)
        values_new = high[:, half_q:].reshape(seq_part, steps, -1, DH).astype(jnp.bfloat16)
        ss = slice(h * seq_part, (h + 1) * seq_part)
        attended = attend(
            queries, keys_new, values_new, cache_keys[ss], cache_values[ss], lengths
        )

        attended = attended.reshape(cols, part // cols, -1)
        turned = []
        for j in range(cols):
            block = lax.dynamic_index_in_dim(attended, t ^ j, 0, keepdims=False)
            turned.append(lax.ppermute(block, "tp", tp_pairs[j]) if j else block)
        turned = jnp.stack(turned)
        heads = []
        for k in range(planes):
            block = lax.dynamic_index_in_dim(turned, t ^ z ^ k, 0, keepdims=False)
            heads.append(lax.ppermute(block, "z", plane_pairs[k]) if k else block)
        heads = jnp.stack(heads)
        piece = part // cols
        gathered = [lax.ppermute(heads, "tp", tp_pairs[j]) if j else heads for j in range(cols)]
        crossed = [lax.ppermute(block, "core", core_pairs) for block in gathered]
        lows, highs = [], []
        for group in GROUPS(cols):
            total = None
            for k in list(range(1, planes)) + [0]:
                block = jnp.concatenate(
                    [gathered[j][k] for j in group] + [crossed[j][k] for j in group]
                )
                product = jnp.dot(block, output_weights, preferred_element_type=jnp.float32)
                if k:
                    product = lax.ppermute(product.astype(jnp.bfloat16), "z", plane_pairs[k])
                    product = product.astype(jnp.float32)
                total = product if total is None else total + product
            total = total.astype(jnp.bfloat16)
            here, there = jnp.split(total, 2)
            there = lax.ppermute(there, "core", core_pairs)
            lows.append(jnp.where(core == 0, here, there))
            highs.append(jnp.where(core == 0, there, here))
        low, high = jnp.concatenate(lows), jnp.concatenate(highs)
        full = jnp.concatenate((low, high), 1).reshape(cols, part // cols, -1)
        full = jnp.stack(by_xor([full[j] for j in range(cols)], t))
        outs.append(full.reshape(seq_part, steps, -1))
    return jnp.concatenate(outs)


def solution(mesh):
    tp_size = mesh.shape["tp"]
    fine = Mesh(mesh.devices.reshape(-1, 2, tp_size), ("z", "core", "tp"))
    fsdp = ("z", "core")
    split = ("z", "core", "tp")
    in_specs = (
        P(fsdp, None, None),
        P(),
        P(split, None),
        P(split, None),
        P(split, None),
        P(split, None),
        P(None, split, None),
        P(),
        P(None, split, None),
        P(),
        P(None, split, None),
        P(),
        P(None, split, None),
        P(),
        P(),
        P(fsdp),
        P(fsdp, None, "tp", None),
        P(fsdp, None, "tp", None),
    )
    out_specs = P(fsdp, None, "tp")
    return jax.shard_map(local, mesh=fine, in_specs=in_specs, out_specs=out_specs, check_vma=False)
```

```python
import functools

import jax
import jax.numpy as jnp
from jax import lax
from jax.experimental import pallas as pl
from jax.experimental.pallas import tpu as pltpu
from jax.sharding import Mesh, PartitionSpec as P

HQ = 64
KVH = 8
DH = 128

rope_theta = 1000000.0
low_rank_scale = 0.5
epsilon = 1e-06
CHUNKS = 2
WIRE = jnp.float16
VMEM_BYTES = 60 * 1024 * 1024


def merge_block(base, down, up):
    delta = lax.dot_general(
        down, up, (((0,), (0,)), ((), ())), preferred_element_type=jnp.float32
    )
    return (base.astype(jnp.float32) + low_rank_scale * delta).astype(jnp.bfloat16)


def merge_kernel(slot_ref, base_ref, down_ref, up_ref, out_ref):
    cores, _, _, piece = out_ref.shape
    for c in range(cores):
        part = slice(c * piece, (c + 1) * piece)
        out_ref[c, 0] = merge_block(base_ref[:, part], down_ref[0], up_ref[0, :, part])


def merge_input_kernel(
    slot_ref, qb_ref, kb_ref, vb_ref, qd_ref, kd_ref, vd_ref, qu_ref, ku_ref, vu_ref, out_ref
):
    cores = out_ref.shape[0]
    piece = qb_ref.shape[1] // cores
    for c in range(cores):
        part = slice(c * piece, (c + 1) * piece)
        out_ref[c, 0, :, :piece] = merge_block(qb_ref[:, part], qd_ref[0], qu_ref[0, :, part])
    out_ref[0, 0, :, piece:] = merge_block(kb_ref[...], kd_ref[0], ku_ref[0])
    out_ref[1, 0, :, piece:] = merge_block(vb_ref[...], vd_ref[0], vu_ref[0])


def flipped(down):
    return jnp.swapaxes(down, 1, 2)


def merge_output(slot, base, down, up, cores, cols):
    depth, width = base.shape
    rank = up.shape[1]
    piece = width // (cols * cores)
    grid = pltpu.PrefetchScalarGridSpec(
        num_scalar_prefetch=1,
        grid=(cols,),
        in_specs=[
            pl.BlockSpec((depth, piece * cores), lambda t, s: (0, t)),
            pl.BlockSpec((1, rank, depth), lambda t, s: (s[0], 0, 0)),
            pl.BlockSpec((1, rank, piece * cores), lambda t, s: (s[0], 0, t)),
        ],
        out_specs=pl.BlockSpec((cores, 1, depth, piece), lambda t, s: (0, t, 0, 0)),
    )
    return pl.pallas_call(
        merge_kernel,
        grid_spec=grid,
        out_shape=jax.ShapeDtypeStruct((cores, cols, depth, piece), base.dtype),
        cost_estimate=pl.CostEstimate(
            flops=2 * depth * rank * width, bytes_accessed=5 * depth * width, transcendentals=0
        ),
        compiler_params=pltpu.CompilerParams(vmem_limit_bytes=VMEM_BYTES),
        name="merge_output",
    )(slot, base, flipped(down), up)


def merge_inputs(slot, bases, downs, ups, cores, cols):
    depth, width = bases[0].shape
    rank = ups[0].shape[1]
    piece = width // (cols * cores)
    side = bases[1].shape[1] // cols
    whole = pl.BlockSpec((1, rank, depth), lambda t, s: (s[0], 0, 0))
    grid = pltpu.PrefetchScalarGridSpec(
        num_scalar_prefetch=1,
        grid=(cols,),
        in_specs=[
            pl.BlockSpec((depth, piece * cores), lambda t, s: (0, t)),
            pl.BlockSpec((depth, side), lambda t, s: (0, t)),
            pl.BlockSpec((depth, side), lambda t, s: (0, t)),
            whole,
            whole,
            whole,
            pl.BlockSpec((1, rank, piece * cores), lambda t, s: (s[0], 0, t)),
            pl.BlockSpec((1, rank, side), lambda t, s: (s[0], 0, t)),
            pl.BlockSpec((1, rank, side), lambda t, s: (s[0], 0, t)),
        ],
        out_specs=pl.BlockSpec((cores, 1, depth, piece + side), lambda t, s: (0, t, 0, 0)),
    )
    return pl.pallas_call(
        merge_input_kernel,
        grid_spec=grid,
        out_shape=jax.ShapeDtypeStruct((cores, cols, depth, piece + side), bases[0].dtype),
        cost_estimate=pl.CostEstimate(
            flops=3 * depth * rank * width, bytes_accessed=6 * depth * width, transcendentals=0
        ),
        compiler_params=pltpu.CompilerParams(vmem_limit_bytes=VMEM_BYTES),
        name="merge_inputs",
    )(slot, *bases, *[flipped(d) for d in downs], *ups)


def norm_kernel(z_ref, x_ref, gain_ref, *refs):
    outs, scratch = refs[:-1], refs[-1]
    x = x_ref[...].astype(jnp.float32)
    mean = jnp.mean(x * x, axis=-1, keepdims=True)
    scratch[...] = (x * lax.rsqrt(mean + epsilon) * gain_ref[...]).astype(jnp.bfloat16)
    block = outs[0].shape[1]
    for k, out_ref in enumerate(outs):
        start = pl.multiple_of((z_ref[0] ^ k) * block, block)
        out_ref[...] = scratch[:, pl.ds(start, block)]


def normed_blocks(z, x, gain, planes):
    rows, width = x.shape
    step = min(rows, 32)
    block = width // planes
    grid = pltpu.PrefetchScalarGridSpec(
        num_scalar_prefetch=1,
        grid=(rows // step,),
        in_specs=[
            pl.BlockSpec((step, width), lambda i, z: (i, 0)),
            pl.BlockSpec((1, width), lambda i, z: (0, 0)),
        ],
        out_specs=[pl.BlockSpec((step, block), lambda i, z: (i, 0))] * planes,
        scratch_shapes=[pltpu.VMEM((step, width), jnp.bfloat16)],
    )
    return pl.pallas_call(
        norm_kernel,
        grid_spec=grid,
        out_shape=[jax.ShapeDtypeStruct((rows, block), jnp.bfloat16)] * planes,
        cost_estimate=pl.CostEstimate(
            flops=6 * rows * width, bytes_accessed=4 * rows * width, transcendentals=rows
        ),
        name="normed_blocks",
    )(z.astype(jnp.int32).reshape(1), x, gain.reshape(1, width))


def rotate(vectors, positions):
    head_dim = vectors.shape[-1]
    half_dim = head_dim // 2
    frequency = rope_theta ** (-2.0 * jnp.arange(half_dim, dtype=jnp.float32) / head_dim)
    phases = positions[:, :, None] * frequency[None, None, :]
    cosine = jnp.concatenate((jnp.cos(phases), jnp.cos(phases)), -1)[:, :, None, :]
    sine = jnp.concatenate((jnp.sin(phases), jnp.sin(phases)), -1)[:, :, None, :]
    turned = jnp.concatenate((-vectors[..., half_dim:], vectors[..., :half_dim]), -1)
    return vectors * cosine + turned * sine


def attend(queries, keys_new, values_new, cache_k, cache_v, lengths):
    seq_count, step_count, head_count, head_dim = queries.shape
    kv_count = keys_new.shape[2]
    grouped = queries.reshape(seq_count, step_count, kv_count, head_count // kv_count, head_dim)
    score_scale = head_dim ** (-0.5)
    old_scores = (
        jnp.einsum("bskgd,blkd->bskgl", grouped, cache_k, preferred_element_type=jnp.float32)
        * score_scale
    )
    new_scores = (
        jnp.einsum("bskgd,btkd->bskgt", grouped, keys_new, preferred_element_type=jnp.float32)
        * score_scale
    )
    live_slots = jnp.arange(cache_k.shape[1], dtype=jnp.int32)[None, :] < lengths[:, None]
    old_scores = jnp.where(live_slots[:, None, None, None, :], old_scores, -1e30)
    causal = jnp.arange(step_count)[:, None] >= jnp.arange(step_count)[None, :]
    new_scores = jnp.where(causal[None, :, None, None, :], new_scores, -1e30)
    highest = jnp.maximum(jnp.max(old_scores, -1), jnp.max(new_scores, -1))[..., None]
    old_exp = jnp.exp(old_scores - highest)
    new_exp = jnp.exp(new_scores - highest)
    denominator = jnp.sum(old_exp, -1, keepdims=True) + jnp.sum(new_exp, -1, keepdims=True)
    old_weights = (old_exp / denominator).astype(jnp.bfloat16)
    new_weights = (new_exp / denominator).astype(jnp.bfloat16)
    mixture = jnp.einsum(
        "bskgl,blkd->bskgd", old_weights, cache_v, preferred_element_type=jnp.float32
    )
    mixture = mixture + jnp.einsum(
        "bskgt,btkd->bskgd", new_weights, values_new, preferred_element_type=jnp.float32
    )
    return mixture.astype(jnp.bfloat16).reshape(seq_count * step_count, head_count * head_dim)


def product_kernel(counts, waits, *refs):
    total = sum(counts)
    ins, weight_ref = refs[:total], refs[total]
    outs, rows_ref = refs[total + 1 + waits : -1], refs[-1]

    @pl.when(pl.program_id(0) == 0)
    def _():
        place = 0
        for ref in ins:
            rows_ref[place : place + ref.shape[0], :] = ref[...]
            place += ref.shape[0]

    product = jnp.dot(rows_ref[...], weight_ref[...], preferred_element_type=jnp.float32)
    place = 0
    for out_ref in outs:
        out_ref[...] = product[place : place + out_ref.shape[0]].astype(out_ref.dtype)
        place += out_ref.shape[0]


def products(groups, weights, kind, after=()):
    depth, width = weights.shape
    tile = 256 if width % 256 == 0 else 128
    counts = [len(group) for group in groups]
    blocks = [block for group in groups for block in group]
    sizes = [sum(block.shape[0] for block in group) for group in groups]
    return pl.pallas_call(
        functools.partial(product_kernel, counts, len(after)),
        grid=(width // tile,),
        in_specs=[pl.BlockSpec(block.shape, lambda i: (0, 0)) for block in blocks]
        + [pl.BlockSpec((depth, tile), lambda i: (0, i))]
        + [pl.BlockSpec(memory_space=pl.ANY)] * len(after),
        out_specs=[pl.BlockSpec((size, tile), lambda i: (0, i)) for size in sizes],
        out_shape=[jax.ShapeDtypeStruct((size, width), kind) for size in sizes],
        scratch_shapes=[pltpu.VMEM((sum(sizes), depth), jnp.bfloat16)],
        compiler_params=pltpu.CompilerParams(vmem_limit_bytes=40 * 1024 * 1024),
        cost_estimate=pl.CostEstimate(flops=1, bytes_accessed=1, transcendentals=0),
        name="products",
    )(*blocks, weights, *after)


def by_xor(blocks, index):
    count = len(blocks)
    bit = 1
    while bit < count:
        odd = (index & bit) != 0
        blocks = [jnp.where(odd, blocks[i ^ bit], blocks[i]) for i in range(count)]
        bit *= 2
    return blocks


def local(
    states,
    norm_gain,
    query_base,
    key_base,
    value_base,
    output_base,
    query_down,
    query_up,
    key_down,
    key_up,
    value_down,
    value_up,
    output_down,
    output_up,
    adapter_layer,
    kv_lengths,
    cache_keys,
    cache_values,
):
    planes, cores, cols = lax.axis_size("z"), lax.axis_size("core"), lax.axis_size("tp")
    z, t = lax.axis_index("z"), lax.axis_index("tp")
    core = lax.axis_index("core")
    plane_pairs = [[(a, a ^ k) for a in range(planes)] for k in range(planes)]
    tp_pairs = [[(a, a ^ k) for a in range(cols)] for k in range(cols)]
    core_pairs = [(0, 1), (1, 0)]
    depth = query_base.shape[0]
    seqs, steps, width = states.shape
    rows = seqs * steps

    joined = merge_inputs(
        adapter_layer,
        (query_base, key_base, value_base),
        (query_down, key_down, value_down),
        (query_up, key_up, value_up),
        cores,
        cols,
    )
    joined, states = lax.optimization_barrier((joined, states))
    joined = joined.reshape(cores * cols * depth, -1)
    weights = lax.all_to_all(joined, ("core", "tp"), 0, 0, tiled=True)
    blocks = normed_blocks(z, states.reshape(rows, width), norm_gain, planes)
    (output_base, *blocks) = lax.optimization_barrier((output_base, *blocks))
    mine = {0: blocks[0]}
    for k in reversed(range(1, planes)):
        mine[k] = lax.ppermute(blocks[k], "z", plane_pairs[k])
    mine = [mine[k] for k in range(planes)]
    other = [lax.ppermute(block, "core", core_pairs) for block in mine]
    merged = merge_output(adapter_layer, output_base, output_down, output_up, cores, cols)
    merged = merged.reshape(cores * cols * depth, -1)
    (weights, merged, *both) = lax.optimization_barrier((weights, merged, *mine, *other))
    mine, other = both[:planes], both[planes:]
    output_weights = lax.all_to_all(merged, ("core", "tp"), 0, 0, tiled=True)

    half_q = HQ * DH // (cols * cores)
    part = rows // CHUNKS
    seq_part = seqs // CHUNKS
    sums = []
    sent = list(reversed(range(1, planes)))
    before = []
    for h in range(CHUNKS):
        sl = slice(h * part, (h + 1) * part)
        pieces = [[mine[k][sl], other[k][sl]] for k in sent]
        terms = products(pieces, weights, jnp.float32, before[:1])
        before = terms
        terms = [lax.ppermute(x.astype(WIRE), "z", plane_pairs[k]) for k, x in zip(sent, terms)]
        sums.append(terms)
    attended = None
    crossing = []
    for h in range(CHUNKS):
        sl = slice(h * part, (h + 1) * part)
        waits = (before[0], output_weights) if attended is None else (attended,)
        terms = sums[h]
        (total,) = products([[mine[0][sl], other[0][sl]]], weights, jnp.float32, waits)
        for term in terms:
            total = total + term.astype(jnp.float32)
        here = total[:part]
        there = lax.ppermute(total[part:], "core", core_pairs)
        low = jnp.where(core == 0, here, there)
        high = jnp.where(core == 0, there, here)
        lengths = kv_lengths[h * seq_part : (h + 1) * seq_part]
        positions = (
            lengths.astype(jnp.float32)[:, None] + jnp.arange(steps, dtype=jnp.float32)[None, :]
        )
        queries = jnp.concatenate((low[:, :half_q], high[:, :half_q]), 1)
        queries = rotate(queries.reshape(seq_part, steps, -1, DH), positions).astype(jnp.bfloat16)
        keys_new = rotate(low[:, half_q:].reshape(seq_part, steps, -1, DH), positions)
        keys_new = keys_new.astype(jnp.bfloat16)
        values_new = high[:, half_q:].reshape(seq_part, steps, -1, DH).astype(jnp.bfloat16)
        ss = slice(h * seq_part, (h + 1) * seq_part)
        attended = attend(
            queries, keys_new, values_new, cache_keys[ss], cache_values[ss], lengths
        )

        quarters = attended.reshape(cols, part // cols, -1)
        turned = []
        for j in range(cols):
            block = lax.dynamic_index_in_dim(quarters, t ^ j, 0, keepdims=False)
            turned.append(lax.ppermute(block, "tp", tp_pairs[j]) if j else block)
        turned = jnp.stack(turned)
        heads = []
        for k in range(planes):
            block = lax.dynamic_index_in_dim(turned, t ^ z ^ k, 0, keepdims=False)
            heads.append(lax.ppermute(block, "z", plane_pairs[k]) if k else block)
        held = jnp.stack(heads)
        gathered = [lax.ppermute(held, "tp", tp_pairs[j]) if j else held for j in range(cols)]
        crossed = [lax.ppermute(block, "core", core_pairs) for block in gathered]
        pieces = [
            [side[j][k] for side in (gathered, crossed) for j in range(cols)]
            for k in range(planes)
        ]
        terms = products([pieces[k] for k in sent], output_weights, jnp.bfloat16)
        crossing.append(
            (pieces[0], terms, [lax.ppermute(x, "z", plane_pairs[k]) for k, x in zip(sent, terms)])
        )
    outs = []
    after = crossing[-1][1]
    for own, _, terms in crossing:
        (total,) = products([own], output_weights, jnp.float32, after[:1])
        for term in terms:
            total = total + term.astype(jnp.float32)
        total = total.astype(jnp.bfloat16)
        here = total[:part]
        there = lax.ppermute(total[part:], "core", core_pairs)
        low = jnp.where(core == 0, here, there)
        high = jnp.where(core == 0, there, here)
        full = jnp.concatenate((low, high), 1).reshape(cols, part // cols, -1)
        full = jnp.stack(by_xor([full[j] for j in range(cols)], t))
        outs.append(full.reshape(seq_part, steps, -1))
    return jnp.concatenate(outs)


def solution(mesh):
    tp_size = mesh.shape["tp"]
    fine = Mesh(mesh.devices.reshape(-1, 2, tp_size), ("z", "core", "tp"))
    fsdp = ("z", "core")
    split = ("z", "core", "tp")
    in_specs = (
        P(fsdp, None, None),
        P(),
        P(split, None),
        P(split, None),
        P(split, None),
        P(split, None),
        P(None, split, None),
        P(),
        P(None, split, None),
        P(),
        P(None, split, None),
        P(),
        P(None, split, None),
        P(),
        P(),
        P(fsdp),
        P(fsdp, None, "tp", None),
        P(fsdp, None, "tp", None),
    )
    out_specs = P(fsdp, None, "tp")
    return jax.shard_map(local, mesh=fine, in_specs=in_specs, out_specs=out_specs, check_vma=False)
```

```python
import functools

import jax
import jax.numpy as jnp
from jax import lax
from jax.experimental import pallas as pl
from jax.experimental.pallas import tpu as pltpu
from jax.sharding import Mesh, PartitionSpec as P

HQ = 64
KVH = 8
DH = 128

rope_theta = 1000000.0
low_rank_scale = 0.5
epsilon = 1e-06
CHUNKS = 2
WIRE = jnp.float16
VMEM_BYTES = 60 * 1024 * 1024


def merge_block(base, down, up):
    delta = lax.dot_general(
        down, up, (((0,), (0,)), ((), ())), preferred_element_type=jnp.float32
    )
    return (base.astype(jnp.float32) + low_rank_scale * delta).astype(jnp.bfloat16)


def merge_kernel(slot_ref, base_ref, down_ref, up_ref, out_ref):
    cores, _, _, piece = out_ref.shape
    for c in range(cores):
        part = slice(c * piece, (c + 1) * piece)
        out_ref[c, 0] = merge_block(base_ref[:, part], down_ref[0], up_ref[0, :, part])


def merge_input_kernel(
    slot_ref, qb_ref, kb_ref, vb_ref, qd_ref, kd_ref, vd_ref, qu_ref, ku_ref, vu_ref, out_ref
):
    cores = out_ref.shape[0]
    piece = qb_ref.shape[1] // cores
    for c in range(cores):
        part = slice(c * piece, (c + 1) * piece)
        out_ref[c, 0, :, :piece] = merge_block(qb_ref[:, part], qd_ref[0], qu_ref[0, :, part])
    out_ref[0, 0, :, piece:] = merge_block(kb_ref[...], kd_ref[0], ku_ref[0])
    out_ref[1, 0, :, piece:] = merge_block(vb_ref[...], vd_ref[0], vu_ref[0])


def flipped(down):
    return jnp.swapaxes(down, 1, 2)


def merge_output(slot, base, down, up, cores, cols):
    depth, width = base.shape
    rank = up.shape[1]
    piece = width // (cols * cores)
    grid = pltpu.PrefetchScalarGridSpec(
        num_scalar_prefetch=1,
        grid=(cols,),
        in_specs=[
            pl.BlockSpec((depth, piece * cores), lambda t, s: (0, t)),
            pl.BlockSpec((1, rank, depth), lambda t, s: (s[0], 0, 0)),
            pl.BlockSpec((1, rank, piece * cores), lambda t, s: (s[0], 0, t)),
        ],
        out_specs=pl.BlockSpec((cores, 1, depth, piece), lambda t, s: (0, t, 0, 0)),
    )
    return pl.pallas_call(
        merge_kernel,
        grid_spec=grid,
        out_shape=jax.ShapeDtypeStruct((cores, cols, depth, piece), base.dtype),
        cost_estimate=pl.CostEstimate(
            flops=2 * depth * rank * width, bytes_accessed=5 * depth * width, transcendentals=0
        ),
        compiler_params=pltpu.CompilerParams(vmem_limit_bytes=VMEM_BYTES),
        name="merge_output",
    )(slot, base, flipped(down), up)


def merge_inputs(slot, bases, downs, ups, cores, cols):
    depth, width = bases[0].shape
    rank = ups[0].shape[1]
    piece = width // (cols * cores)
    side = bases[1].shape[1] // cols
    whole = pl.BlockSpec((1, rank, depth), lambda t, s: (s[0], 0, 0))
    grid = pltpu.PrefetchScalarGridSpec(
        num_scalar_prefetch=1,
        grid=(cols,),
        in_specs=[
            pl.BlockSpec((depth, piece * cores), lambda t, s: (0, t)),
            pl.BlockSpec((depth, side), lambda t, s: (0, t)),
            pl.BlockSpec((depth, side), lambda t, s: (0, t)),
            whole,
            whole,
            whole,
            pl.BlockSpec((1, rank, piece * cores), lambda t, s: (s[0], 0, t)),
            pl.BlockSpec((1, rank, side), lambda t, s: (s[0], 0, t)),
            pl.BlockSpec((1, rank, side), lambda t, s: (s[0], 0, t)),
        ],
        out_specs=pl.BlockSpec((cores, 1, depth, piece + side), lambda t, s: (0, t, 0, 0)),
    )
    return pl.pallas_call(
        merge_input_kernel,
        grid_spec=grid,
        out_shape=jax.ShapeDtypeStruct((cores, cols, depth, piece + side), bases[0].dtype),
        cost_estimate=pl.CostEstimate(
            flops=3 * depth * rank * width, bytes_accessed=6 * depth * width, transcendentals=0
        ),
        compiler_params=pltpu.CompilerParams(vmem_limit_bytes=VMEM_BYTES),
        name="merge_inputs",
    )(slot, *bases, *[flipped(d) for d in downs], *ups)


def norm_kernel(z_ref, x_ref, gain_ref, *refs):
    outs, scratch = refs[:-1], refs[-1]
    x = x_ref[...].astype(jnp.float32)
    mean = jnp.mean(x * x, axis=-1, keepdims=True)
    scratch[...] = (x * lax.rsqrt(mean + epsilon) * gain_ref[...]).astype(jnp.bfloat16)
    block = outs[0].shape[1]
    for k, out_ref in enumerate(outs):
        start = pl.multiple_of((z_ref[0] ^ k) * block, block)
        out_ref[...] = scratch[:, pl.ds(start, block)]


def normed_blocks(z, x, gain, planes):
    rows, width = x.shape
    step = min(rows, 32)
    block = width // planes
    grid = pltpu.PrefetchScalarGridSpec(
        num_scalar_prefetch=1,
        grid=(rows // step,),
        in_specs=[
            pl.BlockSpec((step, width), lambda i, z: (i, 0)),
            pl.BlockSpec((1, width), lambda i, z: (0, 0)),
        ],
        out_specs=[pl.BlockSpec((step, block), lambda i, z: (i, 0))] * planes,
        scratch_shapes=[pltpu.VMEM((step, width), jnp.bfloat16)],
    )
    return pl.pallas_call(
        norm_kernel,
        grid_spec=grid,
        out_shape=[jax.ShapeDtypeStruct((rows, block), jnp.bfloat16)] * planes,
        cost_estimate=pl.CostEstimate(
            flops=6 * rows * width, bytes_accessed=4 * rows * width, transcendentals=rows
        ),
        name="normed_blocks",
    )(z.astype(jnp.int32).reshape(1), x, gain.reshape(1, width))


def rotate(vectors, positions):
    head_dim = vectors.shape[-1]
    half_dim = head_dim // 2
    frequency = rope_theta ** (-2.0 * jnp.arange(half_dim, dtype=jnp.float32) / head_dim)
    phases = positions[:, :, None] * frequency[None, None, :]
    cosine = jnp.concatenate((jnp.cos(phases), jnp.cos(phases)), -1)[:, :, None, :]
    sine = jnp.concatenate((jnp.sin(phases), jnp.sin(phases)), -1)[:, :, None, :]
    turned = jnp.concatenate((-vectors[..., half_dim:], vectors[..., :half_dim]), -1)
    return vectors * cosine + turned * sine


def attend(queries, keys_new, values_new, cache_k, cache_v, lengths):
    seq_count, step_count, head_count, head_dim = queries.shape
    kv_count = keys_new.shape[2]
    grouped = queries.reshape(seq_count, step_count, kv_count, head_count // kv_count, head_dim)
    score_scale = head_dim ** (-0.5)
    old_scores = (
        jnp.einsum("bskgd,blkd->bskgl", grouped, cache_k, preferred_element_type=jnp.float32)
        * score_scale
    )
    new_scores = (
        jnp.einsum("bskgd,btkd->bskgt", grouped, keys_new, preferred_element_type=jnp.float32)
        * score_scale
    )
    live_slots = jnp.arange(cache_k.shape[1], dtype=jnp.int32)[None, :] < lengths[:, None]
    old_scores = jnp.where(live_slots[:, None, None, None, :], old_scores, -1e30)
    causal = jnp.arange(step_count)[:, None] >= jnp.arange(step_count)[None, :]
    new_scores = jnp.where(causal[None, :, None, None, :], new_scores, -1e30)
    highest = jnp.maximum(jnp.max(old_scores, -1), jnp.max(new_scores, -1))[..., None]
    old_exp = jnp.exp(old_scores - highest)
    new_exp = jnp.exp(new_scores - highest)
    denominator = jnp.sum(old_exp, -1, keepdims=True) + jnp.sum(new_exp, -1, keepdims=True)
    old_weights = (old_exp / denominator).astype(jnp.bfloat16)
    new_weights = (new_exp / denominator).astype(jnp.bfloat16)
    mixture = jnp.einsum(
        "bskgl,blkd->bskgd", old_weights, cache_v, preferred_element_type=jnp.float32
    )
    mixture = mixture + jnp.einsum(
        "bskgt,btkd->bskgd", new_weights, values_new, preferred_element_type=jnp.float32
    )
    return mixture.astype(jnp.bfloat16).reshape(seq_count * step_count, head_count * head_dim)


def product_kernel(counts, waits, *refs):
    total = sum(counts)
    ins, weight_ref = refs[:total], refs[total]
    outs, rows_ref = refs[total + 1 + waits : -1], refs[-1]

    @pl.when(pl.program_id(0) == 0)
    def _():
        place = 0
        for ref in ins:
            rows_ref[place : place + ref.shape[0], :] = ref[...]
            place += ref.shape[0]

    product = jnp.dot(rows_ref[...], weight_ref[...], preferred_element_type=jnp.float32)
    place = 0
    for out_ref in outs:
        out_ref[...] = product[place : place + out_ref.shape[0]].astype(out_ref.dtype)
        place += out_ref.shape[0]


def products(groups, weights, kind, after=()):
    depth, width = weights.shape
    tile = 256 if width % 256 == 0 else 128
    counts = [len(group) for group in groups]
    blocks = [block for group in groups for block in group]
    sizes = [sum(block.shape[0] for block in group) for group in groups]
    return pl.pallas_call(
        functools.partial(product_kernel, counts, len(after)),
        grid=(width // tile,),
        in_specs=[pl.BlockSpec(block.shape, lambda i: (0, 0)) for block in blocks]
        + [pl.BlockSpec((depth, tile), lambda i: (0, i))]
        + [pl.BlockSpec(memory_space=pl.ANY)] * len(after),
        out_specs=[pl.BlockSpec((size, tile), lambda i: (0, i)) for size in sizes],
        out_shape=[jax.ShapeDtypeStruct((size, width), kind) for size in sizes],
        scratch_shapes=[pltpu.VMEM((sum(sizes), depth), jnp.bfloat16)],
        compiler_params=pltpu.CompilerParams(vmem_limit_bytes=40 * 1024 * 1024),
        cost_estimate=pl.CostEstimate(flops=1, bytes_accessed=1, transcendentals=0),
        name="products",
    )(*blocks, weights, *after)


def gate_kernel(*refs):
    pass


def gate(x, after):
    return pl.pallas_call(
        gate_kernel,
        in_specs=[pl.BlockSpec(memory_space=pl.ANY)] * (1 + len(after)),
        out_specs=pl.BlockSpec(memory_space=pl.ANY),
        out_shape=jax.ShapeDtypeStruct(x.shape, x.dtype),
        input_output_aliases={0: 0},
        cost_estimate=pl.CostEstimate(flops=1, bytes_accessed=1, transcendentals=0),
        name="gate",
    )(x, *after)


def by_xor(blocks, index):
    count = len(blocks)
    bit = 1
    while bit < count:
        odd = (index & bit) != 0
        blocks = [jnp.where(odd, blocks[i ^ bit], blocks[i]) for i in range(count)]
        bit *= 2
    return blocks


def local(
    states,
    norm_gain,
    query_base,
    key_base,
    value_base,
    output_base,
    query_down,
    query_up,
    key_down,
    key_up,
    value_down,
    value_up,
    output_down,
    output_up,
    adapter_layer,
    kv_lengths,
    cache_keys,
    cache_values,
):
    planes, cores, cols = lax.axis_size("z"), lax.axis_size("core"), lax.axis_size("tp")
    z, t = lax.axis_index("z"), lax.axis_index("tp")
    core = lax.axis_index("core")
    plane_pairs = [[(a, a ^ k) for a in range(planes)] for k in range(planes)]
    tp_pairs = [[(a, a ^ k) for a in range(cols)] for k in range(cols)]
    core_pairs = [(0, 1), (1, 0)]
    depth = query_base.shape[0]
    seqs, steps, width = states.shape
    rows = seqs * steps

    joined = merge_inputs(
        adapter_layer,
        (query_base, key_base, value_base),
        (query_down, key_down, value_down),
        (query_up, key_up, value_up),
        cores,
        cols,
    )
    joined, states = lax.optimization_barrier((joined, states))
    joined = joined.reshape(cores * cols * depth, -1)
    weights = lax.all_to_all(joined, ("core", "tp"), 0, 0, tiled=True)
    blocks = normed_blocks(z, states.reshape(rows, width), norm_gain, planes)
    (output_base, *blocks) = lax.optimization_barrier((output_base, *blocks))
    mine = {0: blocks[0]}
    for k in reversed(range(1, planes)):
        mine[k] = lax.ppermute(blocks[k], "z", plane_pairs[k])
    mine = [mine[k] for k in range(planes)]
    other = [lax.ppermute(block, "core", core_pairs) for block in mine]
    merged = merge_output(adapter_layer, output_base, output_down, output_up, cores, cols)
    merged = merged.reshape(cores * cols * depth, -1)
    (weights, merged, *both) = lax.optimization_barrier((weights, merged, *mine, *other))
    mine, other = both[:planes], both[planes:]
    output_weights = lax.all_to_all(merged, ("core", "tp"), 0, 0, tiled=True)

    half_q = HQ * DH // (cols * cores)
    part = rows // CHUNKS
    seq_part = seqs // CHUNKS
    sums = []
    sent = list(reversed(range(1, planes)))
    before = []
    for h in range(CHUNKS):
        sl = slice(h * part, (h + 1) * part)
        pieces = [[mine[k][sl], other[k][sl]] for k in sent]
        terms = products(pieces, weights, jnp.float32, before[:1])
        before = terms
        terms = [lax.ppermute(x.astype(WIRE), "z", plane_pairs[k]) for k, x in zip(sent, terms)]
        sums.append(terms)
    attended = None
    crossing = []
    for h in range(CHUNKS):
        sl = slice(h * part, (h + 1) * part)
        waits = (before[0],) if attended is None else (attended,)
        terms = sums[h]
        (total,) = products([[mine[0][sl], other[0][sl]]], weights, jnp.float32, waits)
        for term in terms:
            total = total + term.astype(jnp.float32)
        if attended is None:
            total = gate(total, (before[0], output_weights))
        here = total[:part]
        there = lax.ppermute(total[part:], "core", core_pairs)
        low = jnp.where(core == 0, here, there)
        high = jnp.where(core == 0, there, here)
        lengths = kv_lengths[h * seq_part : (h + 1) * seq_part]
        positions = (
            lengths.astype(jnp.float32)[:, None] + jnp.arange(steps, dtype=jnp.float32)[None, :]
        )
        queries = jnp.concatenate((low[:, :half_q], high[:, :half_q]), 1)
        queries = rotate(queries.reshape(seq_part, steps, -1, DH), positions).astype(jnp.bfloat16)
        keys_new = rotate(low[:, half_q:].reshape(seq_part, steps, -1, DH), positions)
        keys_new = keys_new.astype(jnp.bfloat16)
        values_new = high[:, half_q:].reshape(seq_part, steps, -1, DH).astype(jnp.bfloat16)
        ss = slice(h * seq_part, (h + 1) * seq_part)
        attended = attend(
            queries, keys_new, values_new, cache_keys[ss], cache_values[ss], lengths
        )

        quarters = attended.reshape(cols, part // cols, -1)
        turned = []
        for j in range(cols):
            block = lax.dynamic_index_in_dim(quarters, t ^ j, 0, keepdims=False)
            turned.append(lax.ppermute(block, "tp", tp_pairs[j]) if j else block)
        turned = jnp.stack(turned)
        heads = []
        for k in range(planes):
            block = lax.dynamic_index_in_dim(turned, t ^ z ^ k, 0, keepdims=False)
            heads.append(lax.ppermute(block, "z", plane_pairs[k]) if k else block)
        held = jnp.stack(heads)
        gathered = [lax.ppermute(held, "tp", tp_pairs[j]) if j else held for j in range(cols)]
        crossed = [lax.ppermute(block, "core", core_pairs) for block in gathered]
        pieces = [
            [side[j][k] for side in (gathered, crossed) for j in range(cols)]
            for k in range(planes)
        ]
        terms = products([pieces[k] for k in sent], output_weights, jnp.bfloat16)
        crossing.append(
            (pieces[0], terms, [lax.ppermute(x, "z", plane_pairs[k]) for k, x in zip(sent, terms)])
        )
    outs = []
    after = crossing[-1][1]
    for own, _, terms in crossing:
        (total,) = products([own], output_weights, jnp.float32, after[:1])
        for term in terms:
            total = total + term.astype(jnp.float32)
        total = total.astype(jnp.bfloat16)
        here = total[:part]
        there = lax.ppermute(total[part:], "core", core_pairs)
        low = jnp.where(core == 0, here, there)
        high = jnp.where(core == 0, there, here)
        full = jnp.concatenate((low, high), 1).reshape(cols, part // cols, -1)
        full = jnp.stack(by_xor([full[j] for j in range(cols)], t))
        outs.append(full.reshape(seq_part, steps, -1))
    return jnp.concatenate(outs)


def solution(mesh):
    tp_size = mesh.shape["tp"]
    fine = Mesh(mesh.devices.reshape(-1, 2, tp_size), ("z", "core", "tp"))
    fsdp = ("z", "core")
    split = ("z", "core", "tp")
    in_specs = (
        P(fsdp, None, None),
        P(),
        P(split, None),
        P(split, None),
        P(split, None),
        P(split, None),
        P(None, split, None),
        P(),
        P(None, split, None),
        P(),
        P(None, split, None),
        P(),
        P(None, split, None),
        P(),
        P(),
        P(fsdp),
        P(fsdp, None, "tp", None),
        P(fsdp, None, "tp", None),
    )
    out_specs = P(fsdp, None, "tp")
    return jax.shard_map(local, mesh=fine, in_specs=in_specs, out_specs=out_specs, check_vma=False)
```

```python
import functools

import jax
import jax.numpy as jnp
from jax import lax
from jax.experimental import pallas as pl
from jax.experimental.pallas import tpu as pltpu
from jax.sharding import Mesh, PartitionSpec as P

HQ = 64
KVH = 8
DH = 128

rope_theta = 1000000.0
low_rank_scale = 0.5
epsilon = 1e-06
CHUNKS = 2
WIRE = jnp.float16
VMEM_BYTES = 60 * 1024 * 1024


def merge_block(base, down, up):
    delta = lax.dot_general(
        down, up, (((0,), (0,)), ((), ())), preferred_element_type=jnp.float32
    )
    return (base.astype(jnp.float32) + low_rank_scale * delta).astype(jnp.bfloat16)


def merge_kernel(slot_ref, base_ref, down_ref, up_ref, out_ref):
    cores, _, _, piece = out_ref.shape
    for c in range(cores):
        part = slice(c * piece, (c + 1) * piece)
        out_ref[c, 0] = merge_block(base_ref[:, part], down_ref[0], up_ref[0, :, part])


def merge_input_kernel(
    slot_ref, qb_ref, kb_ref, vb_ref, qd_ref, kd_ref, vd_ref, qu_ref, ku_ref, vu_ref, out_ref
):
    cores = out_ref.shape[0]
    piece = qb_ref.shape[1] // cores
    for c in range(cores):
        part = slice(c * piece, (c + 1) * piece)
        out_ref[c, 0, :, :piece] = merge_block(qb_ref[:, part], qd_ref[0], qu_ref[0, :, part])
    out_ref[0, 0, :, piece:] = merge_block(kb_ref[...], kd_ref[0], ku_ref[0])
    out_ref[1, 0, :, piece:] = merge_block(vb_ref[...], vd_ref[0], vu_ref[0])


def flipped(down):
    return jnp.swapaxes(down, 1, 2)


def merge_output(slot, base, down, up, cores, cols):
    depth, width = base.shape
    rank = up.shape[1]
    piece = width // (cols * cores)
    grid = pltpu.PrefetchScalarGridSpec(
        num_scalar_prefetch=1,
        grid=(cols,),
        in_specs=[
            pl.BlockSpec((depth, piece * cores), lambda t, s: (0, t)),
            pl.BlockSpec((1, rank, depth), lambda t, s: (s[0], 0, 0)),
            pl.BlockSpec((1, rank, piece * cores), lambda t, s: (s[0], 0, t)),
        ],
        out_specs=pl.BlockSpec((cores, 1, depth, piece), lambda t, s: (0, t, 0, 0)),
    )
    return pl.pallas_call(
        merge_kernel,
        grid_spec=grid,
        out_shape=jax.ShapeDtypeStruct((cores, cols, depth, piece), base.dtype),
        cost_estimate=pl.CostEstimate(
            flops=2 * depth * rank * width, bytes_accessed=5 * depth * width, transcendentals=0
        ),
        compiler_params=pltpu.CompilerParams(vmem_limit_bytes=VMEM_BYTES),
        name="merge_output",
    )(slot, base, flipped(down), up)


def merge_inputs(slot, bases, downs, ups, cores, cols):
    depth, width = bases[0].shape
    rank = ups[0].shape[1]
    piece = width // (cols * cores)
    side = bases[1].shape[1] // cols
    whole = pl.BlockSpec((1, rank, depth), lambda t, s: (s[0], 0, 0))
    grid = pltpu.PrefetchScalarGridSpec(
        num_scalar_prefetch=1,
        grid=(cols,),
        in_specs=[
            pl.BlockSpec((depth, piece * cores), lambda t, s: (0, t)),
            pl.BlockSpec((depth, side), lambda t, s: (0, t)),
            pl.BlockSpec((depth, side), lambda t, s: (0, t)),
            whole,
            whole,
            whole,
            pl.BlockSpec((1, rank, piece * cores), lambda t, s: (s[0], 0, t)),
            pl.BlockSpec((1, rank, side), lambda t, s: (s[0], 0, t)),
            pl.BlockSpec((1, rank, side), lambda t, s: (s[0], 0, t)),
        ],
        out_specs=pl.BlockSpec((cores, 1, depth, piece + side), lambda t, s: (0, t, 0, 0)),
    )
    return pl.pallas_call(
        merge_input_kernel,
        grid_spec=grid,
        out_shape=jax.ShapeDtypeStruct((cores, cols, depth, piece + side), bases[0].dtype),
        cost_estimate=pl.CostEstimate(
            flops=3 * depth * rank * width, bytes_accessed=6 * depth * width, transcendentals=0
        ),
        compiler_params=pltpu.CompilerParams(vmem_limit_bytes=VMEM_BYTES),
        name="merge_inputs",
    )(slot, *bases, *[flipped(d) for d in downs], *ups)


def norm_kernel(z_ref, x_ref, gain_ref, *refs):
    outs, scratch = refs[:-1], refs[-1]
    x = x_ref[...].astype(jnp.float32)
    mean = jnp.mean(x * x, axis=-1, keepdims=True)
    scratch[...] = (x * lax.rsqrt(mean + epsilon) * gain_ref[...]).astype(jnp.bfloat16)
    block = outs[0].shape[1]
    for k, out_ref in enumerate(outs):
        start = pl.multiple_of((z_ref[0] ^ k) * block, block)
        out_ref[...] = scratch[:, pl.ds(start, block)]


def normed_blocks(z, x, gain, planes):
    rows, width = x.shape
    step = min(rows, 32)
    block = width // planes
    grid = pltpu.PrefetchScalarGridSpec(
        num_scalar_prefetch=1,
        grid=(rows // step,),
        in_specs=[
            pl.BlockSpec((step, width), lambda i, z: (i, 0)),
            pl.BlockSpec((1, width), lambda i, z: (0, 0)),
        ],
        out_specs=[pl.BlockSpec((step, block), lambda i, z: (i, 0))] * planes,
        scratch_shapes=[pltpu.VMEM((step, width), jnp.bfloat16)],
    )
    return pl.pallas_call(
        norm_kernel,
        grid_spec=grid,
        out_shape=[jax.ShapeDtypeStruct((rows, block), jnp.bfloat16)] * planes,
        cost_estimate=pl.CostEstimate(
            flops=6 * rows * width, bytes_accessed=4 * rows * width, transcendentals=rows
        ),
        name="normed_blocks",
    )(z.astype(jnp.int32).reshape(1), x, gain.reshape(1, width))


def rotate(vectors, positions):
    head_dim = vectors.shape[-1]
    half_dim = head_dim // 2
    frequency = rope_theta ** (-2.0 * jnp.arange(half_dim, dtype=jnp.float32) / head_dim)
    phases = positions[:, :, None] * frequency[None, None, :]
    cosine = jnp.concatenate((jnp.cos(phases), jnp.cos(phases)), -1)[:, :, None, :]
    sine = jnp.concatenate((jnp.sin(phases), jnp.sin(phases)), -1)[:, :, None, :]
    turned = jnp.concatenate((-vectors[..., half_dim:], vectors[..., :half_dim]), -1)
    return vectors * cosine + turned * sine


def attend(queries, keys_new, values_new, cache_k, cache_v, lengths):
    seq_count, step_count, head_count, head_dim = queries.shape
    kv_count = keys_new.shape[2]
    grouped = queries.reshape(seq_count, step_count, kv_count, head_count // kv_count, head_dim)
    score_scale = head_dim ** (-0.5)
    old_scores = (
        jnp.einsum("bskgd,blkd->bskgl", grouped, cache_k, preferred_element_type=jnp.float32)
        * score_scale
    )
    new_scores = (
        jnp.einsum("bskgd,btkd->bskgt", grouped, keys_new, preferred_element_type=jnp.float32)
        * score_scale
    )
    live_slots = jnp.arange(cache_k.shape[1], dtype=jnp.int32)[None, :] < lengths[:, None]
    old_scores = jnp.where(live_slots[:, None, None, None, :], old_scores, -1e30)
    causal = jnp.arange(step_count)[:, None] >= jnp.arange(step_count)[None, :]
    new_scores = jnp.where(causal[None, :, None, None, :], new_scores, -1e30)
    highest = jnp.maximum(jnp.max(old_scores, -1), jnp.max(new_scores, -1))[..., None]
    old_exp = jnp.exp(old_scores - highest)
    new_exp = jnp.exp(new_scores - highest)
    denominator = jnp.sum(old_exp, -1, keepdims=True) + jnp.sum(new_exp, -1, keepdims=True)
    old_weights = (old_exp / denominator).astype(jnp.bfloat16)
    new_weights = (new_exp / denominator).astype(jnp.bfloat16)
    mixture = jnp.einsum(
        "bskgl,blkd->bskgd", old_weights, cache_v, preferred_element_type=jnp.float32
    )
    mixture = mixture + jnp.einsum(
        "bskgt,btkd->bskgd", new_weights, values_new, preferred_element_type=jnp.float32
    )
    return mixture.astype(jnp.bfloat16).reshape(seq_count * step_count, head_count * head_dim)


def product_kernel(counts, waits, *refs):
    total = sum(counts)
    ins, weight_ref = refs[:total], refs[total]
    outs, rows_ref = refs[total + 1 + waits : -1], refs[-1]

    @pl.when(pl.program_id(0) == 0)
    def _():
        place = 0
        for ref in ins:
            rows_ref[place : place + ref.shape[0], :] = ref[...]
            place += ref.shape[0]

    product = jnp.dot(rows_ref[...], weight_ref[...], preferred_element_type=jnp.float32)
    place = 0
    for out_ref in outs:
        out_ref[...] = product[place : place + out_ref.shape[0]].astype(out_ref.dtype)
        place += out_ref.shape[0]


def products(groups, weights, kind, after=()):
    depth, width = weights.shape
    tile = next(n for n in (width // 2, 256, 128) if n % 128 == 0 and width % n == 0)
    counts = [len(group) for group in groups]
    blocks = [block for group in groups for block in group]
    sizes = [sum(block.shape[0] for block in group) for group in groups]
    return pl.pallas_call(
        functools.partial(product_kernel, counts, len(after)),
        grid=(width // tile,),
        in_specs=[pl.BlockSpec(block.shape, lambda i: (0, 0)) for block in blocks]
        + [pl.BlockSpec((depth, tile), lambda i: (0, i))]
        + [pl.BlockSpec(memory_space=pl.ANY)] * len(after),
        out_specs=[pl.BlockSpec((size, tile), lambda i: (0, i)) for size in sizes],
        out_shape=[jax.ShapeDtypeStruct((size, width), kind) for size in sizes],
        scratch_shapes=[pltpu.VMEM((sum(sizes), depth), jnp.bfloat16)],
        compiler_params=pltpu.CompilerParams(vmem_limit_bytes=40 * 1024 * 1024),
        cost_estimate=pl.CostEstimate(flops=1, bytes_accessed=1, transcendentals=0),
        name="products",
    )(*blocks, weights, *after)


def gate_kernel(*refs):
    pass


def gate(x, after):
    return pl.pallas_call(
        gate_kernel,
        in_specs=[pl.BlockSpec(memory_space=pl.ANY)] * (1 + len(after)),
        out_specs=pl.BlockSpec(memory_space=pl.ANY),
        out_shape=jax.ShapeDtypeStruct(x.shape, x.dtype),
        input_output_aliases={0: 0},
        cost_estimate=pl.CostEstimate(flops=1, bytes_accessed=1, transcendentals=0),
        name="gate",
    )(x, *after)


def by_xor(blocks, index):
    count = len(blocks)
    bit = 1
    while bit < count:
        odd = (index & bit) != 0
        blocks = [jnp.where(odd, blocks[i ^ bit], blocks[i]) for i in range(count)]
        bit *= 2
    return blocks


def local(
    states,
    norm_gain,
    query_base,
    key_base,
    value_base,
    output_base,
    query_down,
    query_up,
    key_down,
    key_up,
    value_down,
    value_up,
    output_down,
    output_up,
    adapter_layer,
    kv_lengths,
    cache_keys,
    cache_values,
):
    planes, cores, cols = lax.axis_size("z"), lax.axis_size("core"), lax.axis_size("tp")
    z, t = lax.axis_index("z"), lax.axis_index("tp")
    core = lax.axis_index("core")
    plane_pairs = [[(a, a ^ k) for a in range(planes)] for k in range(planes)]
    tp_pairs = [[(a, a ^ k) for a in range(cols)] for k in range(cols)]
    core_pairs = [(0, 1), (1, 0)]
    depth = query_base.shape[0]
    seqs, steps, width = states.shape
    rows = seqs * steps

    joined = merge_inputs(
        adapter_layer,
        (query_base, key_base, value_base),
        (query_down, key_down, value_down),
        (query_up, key_up, value_up),
        cores,
        cols,
    )
    joined, states = lax.optimization_barrier((joined, states))
    joined = joined.reshape(cores * cols * depth, -1)
    weights = lax.all_to_all(joined, ("core", "tp"), 0, 0, tiled=True)
    blocks = normed_blocks(z, states.reshape(rows, width), norm_gain, planes)
    (output_base, *blocks) = lax.optimization_barrier((output_base, *blocks))
    mine = {0: blocks[0]}
    for k in reversed(range(1, planes)):
        mine[k] = lax.ppermute(blocks[k], "z", plane_pairs[k])
    mine = [mine[k] for k in range(planes)]
    other = [lax.ppermute(block, "core", core_pairs) for block in mine]
    merged = merge_output(adapter_layer, output_base, output_down, output_up, cores, cols)
    merged = merged.reshape(cores * cols * depth, -1)
    (weights, merged, *both) = lax.optimization_barrier((weights, merged, *mine, *other))
    mine, other = both[:planes], both[planes:]
    output_weights = lax.all_to_all(merged, ("core", "tp"), 0, 0, tiled=True)

    half_q = HQ * DH // (cols * cores)
    part = rows // CHUNKS
    seq_part = seqs // CHUNKS
    sums = []
    sent = list(reversed(range(1, planes)))
    before = []
    for h in range(CHUNKS):
        sl = slice(h * part, (h + 1) * part)
        pieces = [[mine[k][sl], other[k][sl]] for k in sent]
        terms = products(pieces, weights, jnp.float32, before[:1])
        before = terms
        terms = [lax.ppermute(x.astype(WIRE), "z", plane_pairs[k]) for k, x in zip(sent, terms)]
        sums.append(terms)
    attended = None
    crossing = []
    for h in range(CHUNKS):
        sl = slice(h * part, (h + 1) * part)
        waits = (before[0],) if attended is None else (attended,)
        terms = sums[h]
        (total,) = products([[mine[0][sl], other[0][sl]]], weights, jnp.float32, waits)
        for term in terms:
            total = total + term.astype(jnp.float32)
        if attended is None:
            total = gate(total, (before[0], output_weights))
        here = total[:part]
        there = lax.ppermute(total[part:], "core", core_pairs)
        low = jnp.where(core == 0, here, there)
        high = jnp.where(core == 0, there, here)
        lengths = kv_lengths[h * seq_part : (h + 1) * seq_part]
        positions = (
            lengths.astype(jnp.float32)[:, None] + jnp.arange(steps, dtype=jnp.float32)[None, :]
        )
        queries = jnp.concatenate((low[:, :half_q], high[:, :half_q]), 1)
        queries = rotate(queries.reshape(seq_part, steps, -1, DH), positions).astype(jnp.bfloat16)
        keys_new = rotate(low[:, half_q:].reshape(seq_part, steps, -1, DH), positions)
        keys_new = keys_new.astype(jnp.bfloat16)
        values_new = high[:, half_q:].reshape(seq_part, steps, -1, DH).astype(jnp.bfloat16)
        ss = slice(h * seq_part, (h + 1) * seq_part)
        attended = attend(
            queries, keys_new, values_new, cache_keys[ss], cache_values[ss], lengths
        )

        quarters = attended.reshape(cols, part // cols, -1)
        turned = []
        for j in range(cols):
            block = lax.dynamic_index_in_dim(quarters, t ^ j, 0, keepdims=False)
            turned.append(lax.ppermute(block, "tp", tp_pairs[j]) if j else block)
        turned = jnp.stack(turned)
        heads = []
        for k in range(planes):
            block = lax.dynamic_index_in_dim(turned, t ^ z ^ k, 0, keepdims=False)
            heads.append(lax.ppermute(block, "z", plane_pairs[k]) if k else block)
        held = jnp.stack(heads)
        gathered = [lax.ppermute(held, "tp", tp_pairs[j]) if j else held for j in range(cols)]
        crossed = [lax.ppermute(block, "core", core_pairs) for block in gathered]
        pieces = [
            [side[j][k] for side in (gathered, crossed) for j in range(cols)]
            for k in range(planes)
        ]
        terms = products([pieces[k] for k in sent], output_weights, jnp.bfloat16)
        crossing.append(
            (pieces[0], terms, [lax.ppermute(x, "z", plane_pairs[k]) for k, x in zip(sent, terms)])
        )
    outs = []
    after = crossing[-1][1]
    for own, _, terms in crossing:
        (total,) = products([own], output_weights, jnp.float32, after[:1])
        for term in terms:
            total = total + term.astype(jnp.float32)
        total = total.astype(jnp.bfloat16)
        here = total[:part]
        there = lax.ppermute(total[part:], "core", core_pairs)
        low = jnp.where(core == 0, here, there)
        high = jnp.where(core == 0, there, here)
        full = jnp.concatenate((low, high), 1).reshape(cols, part // cols, -1)
        full = jnp.stack(by_xor([full[j] for j in range(cols)], t))
        outs.append(full.reshape(seq_part, steps, -1))
    return jnp.concatenate(outs)


def solution(mesh):
    tp_size = mesh.shape["tp"]
    fine = Mesh(mesh.devices.reshape(-1, 2, tp_size), ("z", "core", "tp"))
    fsdp = ("z", "core")
    split = ("z", "core", "tp")
    in_specs = (
        P(fsdp, None, None),
        P(),
        P(split, None),
        P(split, None),
        P(split, None),
        P(split, None),
        P(None, split, None),
        P(),
        P(None, split, None),
        P(),
        P(None, split, None),
        P(),
        P(None, split, None),
        P(),
        P(),
        P(fsdp),
        P(fsdp, None, "tp", None),
        P(fsdp, None, "tp", None),
    )
    out_specs = P(fsdp, None, "tp")
    return jax.shard_map(local, mesh=fine, in_specs=in_specs, out_specs=out_specs, check_vma=False)
```
